256 devices in a mesh: ctx: 32 (over z, y_hi, core), tp: 8 (over y_lo, x).
Axes of the slice: x: 4, y: 4 (y_hi: 2, y_lo: 2; y = y_hi * 2 + y_lo), z: 8, core: 2. Of those that a mesh axis runs over, the one named last changes fastest.
Arguments:
- sample_ids: int32 [128], replicated, may hold values from 0 to 7, never falling along the last dimension, each value on 1 to 32 neighbouring positions
- layer_input: bfloat16 [16384, 8192], P('ctx', 'tp'), may hold values from -6 to 6
- hidden_acts: bfloat16 [16384, 28672], P('ctx', 'tp'), may hold values from -6 to 6
- gate_grad: bfloat16 [16384, 28672], P('ctx', 'tp'), may hold values from -0.1796875 to 0.1796875
- up_grad: bfloat16 [16384, 28672], P('ctx', 'tp'), may hold values from -0.1796875 to 0.1796875
- output_grad: bfloat16 [16384, 8192], P('ctx', 'tp'), may hold values from -0.1796875 to 0.1796875
- input_basis: bfloat16 [8192, 64], P('tp'), may hold values from -0.0625 to 0.0625
- hidden_basis: bfloat16 [28672, 64], P('tp'), may hold values from -0.03125 to 0.03125
- gate_basis: bfloat16 [28672, 64], P('tp'), may hold values from -0.03125 to 0.03125
- up_basis: bfloat16 [28672, 64], P('tp'), may hold values from -0.03125 to 0.03125
- output_basis: bfloat16 [8192, 64], P('tp'), may hold values from -0.0625 to 0.0625
Outputs:
- sample_grads: float32 [3, 8, 4096], P(None, None, 'ctx')
The draws below stay inside these ranges and needn't reach their ends.
Inputs may be any that keep to these rules, and one draw needn't show every extreme that they name: `sample_ids`: sample ids never fall from one block to the next; every sequence holds 1 to 32 blocks, one exactly 32.
All inputs are finite; a program needn't handle non-finite values.
Results may differ from the reference program's by a relative error of at most 0.0003.
Values sent between devices are 32-bit elements; how exact they have to be, the bound alone decides.
A program may use at most 64 MiB of HBM per device.

```python
import math
import jax
import jax.numpy as jnp
import numpy as np
from jax import lax

D = 8192
FF = 28672
K = 64
SAMPLES = 8
BLOCK = 128
TOKENS = 16384
NBLK = 128
BLOCK_MOST = 32


def level_of(key, shape, cuts, low, largest):
    gain = 1.0
    for axis_at, parts in cuts:
        heights = jax.random.uniform(jax.random.fold_in(jax.random.fold_in(key, 6), axis_at), (parts,), jnp.float32, low / len(cuts), largest / len(cuts))
        gain = gain * jnp.repeat(jnp.exp(heights), shape[axis_at] // parts).reshape((-1,) + (1,) * (len(shape) - 1 - axis_at))
    return gain


def length_profile(number_of, total, reach, slope):
    portions = [(1 << 20) // math.isqrt(standing ** slope) + 1 for standing in range(2, number_of + 1)]
    spare, given = total - reach - (number_of - 1), [1] * (number_of - 1)
    while spare > 0:
        candidates = [i for i in range(number_of - 1) if given[i] < reach]
        whole, budget = sum([portions[i] for i in candidates]), spare
        for i in candidates:
            addition = min(reach - given[i], max(1, budget * portions[i] // whole), spare)
            given[i] = given[i] + addition
            spare = spare - addition
    return np.array([reach] + given)


def uneven_parts(own_key, amount, total, reach, skew):
    if amount == 2:
        one = jax.random.randint(own_key, (), max(1, total - reach), min(reach, total - 1) + 1)
        return jnp.stack([one, total - one])
    lengths = jnp.asarray(length_profile(amount, total, reach, skew), jnp.int32)
    pairs = (amount - 1) // 2
    giver, sink = lengths[1:1 + 2 * pairs:2], lengths[2:2 + 2 * pairs:2]
    slack = jnp.minimum(giver - 1, reach - sink)
    passed = jax.random.randint(jax.random.fold_in(own_key, 1), (pairs,), 0, 1 << 20) % (slack + 1)
    lengths = lengths.at[1:1 + 2 * pairs:2].set(giver - passed).at[2:2 + 2 * pairs:2].set(sink + passed)
    return lengths[jax.random.permutation(jax.random.fold_in(own_key, 2), amount)]


def normal_values(rng, dims, scale, limit, cuts=(), kind=jnp.bfloat16):
    entries = scale * jax.random.normal(rng, dims, jnp.float32)
    if cuts:
        entries = entries * level_of(rng, dims, cuts, -0.22, 0.18)
    return jnp.clip(entries, -limit, limit).astype(kind)


def setup_inputs(seed: int = 0) -> dict:
    arg_keys = jax.random.split(jax.random.key(seed), 12)
    return {
        "sample_ids": jnp.searchsorted(jnp.cumsum(uneven_parts(arg_keys[0], SAMPLES, NBLK, BLOCK_MOST, 0)), jnp.arange(NBLK), side="right").astype(jnp.int32),
        "layer_input": normal_values(arg_keys[1], (TOKENS, D), 1.0, 6.0, ((0, 32), (1, 8))),
        "hidden_acts": normal_values(arg_keys[2], (TOKENS, FF), 1.0, 6.0, ((0, 32), (1, 8))),
        "gate_grad": normal_values(arg_keys[3], (TOKENS, FF), 0.03, 0.1796875, ((0, 32), (1, 8))),
        "up_grad": normal_values(arg_keys[4], (TOKENS, FF), 0.03, 0.1796875, ((0, 32), (1, 8))),
        "output_grad": normal_values(arg_keys[5], (TOKENS, D), 0.03, 0.1796875, ((0, 32), (1, 8))),
        "input_basis": normal_values(arg_keys[6], (D, K), D ** -0.5, 0.0625, ((0, 8),)),
        "hidden_basis": normal_values(arg_keys[7], (FF, K), FF ** -0.5, 0.03125, ((0, 8),)),
        "gate_basis": normal_values(arg_keys[8], (FF, K), FF ** -0.5, 0.03125, ((0, 8),)),
        "up_basis": normal_values(arg_keys[9], (FF, K), FF ** -0.5, 0.03125, ((0, 8),)),
        "output_basis": normal_values(arg_keys[10], (D, K), D ** -0.5, 0.0625, ((0, 8),)),
    }


def per_sample(one_hot, output_side, input_side):
    spread = (one_hot[:, :, None] * output_side[:, None, :]).reshape(output_side.shape[0], -1)
    summed = jnp.einsum("ta,tb->ab", spread, input_side, precision=lax.Precision.HIGHEST)
    return summed.reshape(SAMPLES, K * K)


def reference(sample_ids, layer_input, hidden_acts, gate_grad, up_grad, output_grad, input_basis, hidden_basis, gate_basis, up_basis, output_basis):
    in_low = jnp.dot(layer_input, input_basis, preferred_element_type=jnp.float32)
    hid_low = jnp.dot(hidden_acts, hidden_basis, preferred_element_type=jnp.float32)
    gate_low = jnp.dot(gate_grad, gate_basis, preferred_element_type=jnp.float32)
    up_low = jnp.dot(up_grad, up_basis, preferred_element_type=jnp.float32)
    out_low = jnp.dot(output_grad, output_basis, preferred_element_type=jnp.float32)
    owners = jnp.repeat(sample_ids, BLOCK)
    one_hot = (owners[:, None] == jnp.arange(SAMPLES, dtype=jnp.int32)[None, :]).astype(jnp.float32)
    return jnp.stack([per_sample(one_hot, gate_low, in_low), per_sample(one_hot, up_low, in_low), per_sample(one_hot, out_low, hid_low)])
```

```python
import functools

import jax
import jax.numpy as jnp
from jax import lax
from jax.experimental import pallas as pl
from jax.experimental.pallas import tpu as pltpu
from jax.sharding import PartitionSpec as P

K = 64
SAMPLES = 8
BLOCK = 128
LANES = 128
MESH = pl.DeviceIdType.MESH
HIGHEST = lax.Precision.HIGHEST


def project(data_ref, basis_ref):
    return lax.dot_general(
        data_ref[...], basis_ref[...], (((1,), (1,)), ((), ())), preferred_element_type=jnp.float32
    )


def kernel(n_ctx, n_tp, ids, x_in, x_hid, x_gate, x_up, x_out, b_in, b_hid, b_gate, b_up, b_out, result,
           v_in, v_hid, v_gate, v_up, v_out, w_in, w_hid, w_gate, w_up, w_out,
           s_io, s_h, s_gu, r_io, r_h, r_gu, grads, g_send, g_recv, f_recv,
           load_sem, tp_send, tp_recv, ctx_send, ctx_recv, fin_send, fin_recv):
    me_ctx, me_tp = lax.axis_index("ctx"), lax.axis_index("tp")
    own = v_in.shape[0] // n_tp

    loads = []
    pairs = [(x_in, v_in), (b_in, w_in), (x_out, v_out), (b_out, w_out), (x_hid, v_hid), (b_hid, w_hid),
             (x_gate, v_gate), (b_gate, w_gate), (x_up, v_up), (b_up, w_up)]
    for i, (src, dst) in enumerate(pairs):
        load = pltpu.make_async_copy(src, dst, load_sem.at[i])
        load.start()
        loads.append(load)

    barrier = pltpu.get_barrier_semaphore()

    @pl.loop(1, n_tp)
    def _(step):
        pl.semaphore_signal(barrier, inc=1, device_id=(me_ctx, lax.rem(me_tp + step, n_tp)), device_id_type=MESH)

    @pl.loop(1, n_ctx)
    def _(step):
        pl.semaphore_signal(barrier, inc=1, device_id=(lax.rem(me_ctx + step, n_ctx), me_tp), device_id_type=MESH)

    def ready(first):
        loads[first].wait()
        loads[first + 1].wait()

    def exchange(kind, send, recv):
        recv[me_tp] = send[me_tp]

        @pl.loop(1, n_tp)
        def _(step):
            peer = lax.rem(me_tp + step, n_tp)
            pltpu.make_async_remote_copy(
                src_ref=send.at[peer], dst_ref=recv.at[me_tp],
                send_sem=tp_send.at[kind], recv_sem=tp_recv.at[kind],
                device_id=(me_ctx, peer), device_id_type=MESH,
            ).start()

    def finish(kind, send, recv):
        part = recv.at[pl.ds(0, n_tp - 1)]
        pltpu.make_async_copy(part, part, tp_recv.at[kind]).wait()
        part = send.at[pl.ds(0, n_tp - 1)]
        pltpu.make_async_copy(part, part, tp_send.at[kind]).wait()
        total = recv[0]
        for source in range(1, n_tp):
            total = total + recv[source]
        return total

    ready(0)
    low_in = project(v_in, w_in)
    ready(2)
    low_out = project(v_out, w_out)
    s_io[...] = jnp.concatenate([low_in, low_out], axis=1).reshape(s_io.shape)
    pl.semaphore_wait(barrier, n_tp + n_ctx - 2)
    exchange(0, s_io, r_io)

    ready(4)
    low_hid = project(v_hid, w_hid).reshape(n_tp, 2, own // 2, K)
    s_h[...] = jnp.concatenate([low_hid[:, 0], low_hid[:, 1]], axis=2)
    exchange(1, s_h, r_h)

    ready(6)
    low_gate = project(v_gate, w_gate)
    ready(8)
    low_up = project(v_up, w_up)
    s_gu[...] = jnp.concatenate([low_gate, low_up], axis=1).reshape(s_gu.shape)
    exchange(2, s_gu, r_gu)

    in_out = finish(0, s_io, r_io)
    hid_halves = finish(1, s_h, r_h)
    hid = jnp.concatenate([hid_halves[:, :K], hid_halves[:, K:]], axis=0)
    gate_up = finish(2, s_gu, r_gu)

    def outer(output_side, input_side):
        return lax.dot_general(output_side, input_side, (((0,), (0,)), ((), ())), precision=HIGHEST,
                               preferred_element_type=jnp.float32)

    grads[pl.ds(0, 2 * K), :K] = outer(gate_up, in_out[:, :K])
    grads[pl.ds(2 * K, K), :K] = outer(in_out[:, K:], hid)
    even = grads[pl.ds(0, 3 * K // 2, stride=2), :]
    odd = grads[pl.ds(1, 3 * K // 2, stride=2), :]
    both = jnp.concatenate([even[:, :K], odd[:, :K]], axis=1)
    for m in range(3):
        g_send[:, m, :] = both[m * n_ctx:(m + 1) * n_ctx]
    g_recv[me_ctx] = g_send[me_ctx]

    @pl.loop(1, n_ctx)
    def _(step):
        peer = lax.rem(me_ctx + step, n_ctx)
        pltpu.make_async_remote_copy(
            src_ref=g_send.at[peer], dst_ref=g_recv.at[me_ctx],
            send_sem=ctx_send, recv_sem=ctx_recv,
            device_id=(peer, me_tp), device_id_type=MESH,
        ).start()

    part = g_recv.at[pl.ds(0, n_ctx - 1)]
    pltpu.make_async_copy(part, part, ctx_recv).wait()
    part = g_send.at[pl.ds(0, n_ctx - 1)]
    pltpu.make_async_copy(part, part, ctx_send).wait()

    sample = lax.broadcasted_iota(jnp.int32, (SAMPLES, LANES), 0)
    sums = [jnp.zeros((SAMPLES, LANES), jnp.float32) for _ in range(3)]
    blocks = v_in.shape[0] // BLOCK
    mine = me_tp * own // BLOCK
    for source in range(n_ctx):
        chosen = sample == ids[source * blocks + mine]
        for m in range(3):
            row = jnp.broadcast_to(g_recv[source, m:m + 1, :], (SAMPLES, LANES))
            sums[m] = sums[m] + jnp.where(chosen, row, 0.0)
    for m in range(3):
        f_recv[me_tp, m] = sums[m]

    @pl.loop(1, n_tp)
    def _(step):
        peer = lax.rem(me_tp + step, n_tp)
        pltpu.make_async_remote_copy(
            src_ref=f_recv.at[me_tp], dst_ref=f_recv.at[me_tp],
            send_sem=fin_send, recv_sem=fin_recv,
            device_id=(me_ctx, peer), device_id_type=MESH,
        ).start()

    part = f_recv.at[pl.ds(0, n_tp - 1)]
    pltpu.make_async_copy(part, part, fin_recv).wait()
    total = f_recv[0]
    for source in range(1, n_tp):
        total = total + f_recv[source]
    result[...] = total
    pltpu.make_async_copy(part, part, fin_send).wait()


def body(ids, x_in, x_hid, x_gate, x_up, x_out, b_in, b_hid, b_gate, b_up, b_out, *, n_ctx, n_tp):
    tokens, narrow = x_in.shape
    wide = x_hid.shape[1]
    own = tokens // n_tp
    anywhere = pl.BlockSpec(memory_space=pl.ANY)
    f32, bf16 = jnp.float32, jnp.bfloat16
    dma = pltpu.SemaphoreType.DMA
    return pl.pallas_call(
        functools.partial(kernel, n_ctx, n_tp),
        out_shape=jax.ShapeDtypeStruct((3, SAMPLES, LANES), f32),
        in_specs=[pl.BlockSpec(memory_space=pltpu.SMEM)] + [anywhere] * 10,
        out_specs=pl.BlockSpec(memory_space=pltpu.VMEM),
        scratch_shapes=[
            pltpu.VMEM((tokens, narrow), bf16),
            pltpu.VMEM((tokens, wide), bf16),
            pltpu.VMEM((tokens, wide), bf16),
            pltpu.VMEM((tokens, wide), bf16),
            pltpu.VMEM((tokens, narrow), bf16),
            pltpu.VMEM((K, narrow), bf16),
            pltpu.VMEM((K, wide), bf16),
            pltpu.VMEM((K, wide), bf16),
            pltpu.VMEM((K, wide), bf16),
            pltpu.VMEM((K, narrow), bf16),
            pltpu.VMEM((n_tp, own, LANES), f32),
            pltpu.VMEM((n_tp, own // 2, LANES), f32),
            pltpu.VMEM((n_tp, own, LANES), f32),
            pltpu.VMEM((n_tp, own, LANES), f32),
            pltpu.VMEM((n_tp, own // 2, LANES), f32),
            pltpu.VMEM((n_tp, own, LANES), f32),
            pltpu.VMEM((3 * K, LANES), f32),
            pltpu.VMEM((n_ctx, 4, LANES), f32),
            pltpu.VMEM((n_ctx, 4, LANES), f32),
            pltpu.VMEM((n_tp, 3, SAMPLES, LANES), f32),
            dma((10,)), dma((3,)), dma((3,)), dma, dma, dma, dma,
        ],
        compiler_params=pltpu.CompilerParams(
            collective_id=0, has_side_effects=True, vmem_limit_bytes=60 * 1024 * 1024
        ),
    )(ids, x_in, x_hid, x_gate, x_up, x_out, b_in.T, b_hid.T, b_gate.T, b_up.T, b_out.T)


def solution(mesh):
    split, rows = P("ctx", "tp"), P("tp", None)
    return jax.shard_map(
        functools.partial(body, n_ctx=mesh.shape["ctx"], n_tp=mesh.shape["tp"]),
        mesh=mesh,
        in_specs=(P(), split, split, split, split, split, rows, rows, rows, rows, rows),
        out_specs=P(None, None, "ctx"),
        check_vma=False,
    )
```

```python
import functools

import jax
import jax.numpy as jnp
from jax import lax
from jax.experimental import pallas as pl
from jax.experimental.pallas import tpu as pltpu
from jax.sharding import PartitionSpec as P

K = 64
SAMPLES = 8
BLOCK = 128
LANES = 128
MESH = pl.DeviceIdType.MESH
HIGHEST = lax.Precision.HIGHEST


def project(data_ref, basis_ref):
    half = data_ref.shape[0] // 2
    basis = basis_ref[...]
    parts = [
        lax.dot_general(
            data_ref[pl.ds(start, half), :], basis, (((1,), (1,)), ((), ())), preferred_element_type=jnp.float32
        )
        for start in (0, half)
    ]
    return jnp.concatenate(parts, axis=0)


def outer(output_side, input_side):
    return lax.dot_general(
        output_side, input_side, (((0,), (0,)), ((), ())), precision=HIGHEST, preferred_element_type=jnp.float32
    )


def wait_bytes(ref, count, sem):
    part = ref.at[pl.ds(0, count)]
    pltpu.make_async_copy(part, part, sem).wait()


def kernel(n_ctx, n_tp, x_ids, x_in, x_hid, x_gate, x_up, x_out, b_in, b_hid, b_gate, b_up, b_out, result,
           ids, v_in, v_hid, v_gate, v_up, v_out, w_in, w_hid, w_gate, w_up, w_out,
           s_io, s_hg, s_u, r_io, r_hg, r_u, grads_go, grads_u, gs_go, gs_u, gr_go, gr_u, f_go, f_u,
           ids_sem, load_sem, tp_send, tp_recv, ctx_send, ctx_recv, fin_send, fin_recv):
    me_ctx, me_tp = lax.axis_index("ctx"), lax.axis_index("tp")
    tokens = v_in.shape[0]
    own = tokens // n_tp

    loads = []

    def load(src, dst):
        copy = pltpu.make_async_copy(src, dst, load_sem.at[len(loads)])
        copy.start()
        loads.append(copy)

    load(x_in, v_in)
    load(b_in, w_in)
    load(x_out, v_out)
    load(b_out, w_out)
    load(x_hid, v_hid)
    load(b_hid, w_hid)

    barrier = pltpu.get_barrier_semaphore()

    @pl.loop(1, n_ctx)
    def _(step):
        pl.semaphore_signal(barrier, inc=1, device_id=(jnp.bitwise_xor(me_ctx, step), me_tp), device_id_type=MESH)

    @pl.loop(1, n_tp)
    def _(step):
        pl.semaphore_signal(barrier, inc=1, device_id=(me_ctx, jnp.bitwise_xor(me_tp, step)), device_id_type=MESH)

    load(x_gate, v_gate)
    load(b_gate, w_gate)
    load(x_up, v_up)
    load(b_up, w_up)
    ids_copy = pltpu.make_async_copy(x_ids, ids, ids_sem)
    ids_copy.start()

    def ready(first):
        loads[first].wait()
        loads[first + 1].wait()

    def tp_exchange(kind, send, recv):
        @pl.loop(1, n_tp)
        def _(step):
            peer = jnp.bitwise_xor(me_tp, step)
            pltpu.make_async_remote_copy(
                src_ref=send.at[peer], dst_ref=recv.at[me_tp],
                send_sem=tp_send.at[kind], recv_sem=tp_recv.at[kind],
                device_id=(me_ctx, peer), device_id_type=MESH,
            ).start()

        recv[me_tp] = send[me_tp]

    def tp_total(kind, recv):
        wait_bytes(recv, n_tp - 1, tp_recv.at[kind])
        total = recv[0]
        for source in range(1, n_tp):
            total = total + recv[source]
        return total

    def ctx_exchange(kind, send, recv):
        @pl.loop(1, n_ctx)
        def _(step):
            peer = jnp.bitwise_xor(me_ctx, step)
            pltpu.make_async_remote_copy(
                src_ref=send.at[peer], dst_ref=recv.at[me_ctx],
                send_sem=ctx_send.at[kind], recv_sem=ctx_recv.at[kind],
                device_id=(peer, me_tp), device_id_type=MESH,
            ).start()

        recv[me_ctx] = send[me_ctx]

    def slices(grads, send, count):
        even = grads[pl.ds(0, count * K // 2, stride=2), :]
        odd = grads[pl.ds(1, count * K // 2, stride=2), :]
        both = jnp.concatenate([even[:, :K], odd[:, :K]], axis=1)
        for m in range(count):
            send[:, m, :] = both[m * n_ctx:(m + 1) * n_ctx]

    def by_sample(kind, recv, out, count):
        wait_bytes(recv, n_ctx - 1, ctx_recv.at[kind])
        sample = lax.broadcasted_iota(jnp.int32, (SAMPLES, LANES), 0)
        sums = [jnp.zeros((SAMPLES, LANES), jnp.float32) for _ in range(count)]
        blocks = tokens // BLOCK
        mine = me_tp * own // BLOCK
        for source in range(n_ctx):
            chosen = sample == ids[source * blocks + mine]
            for m in range(count):
                row = jnp.broadcast_to(recv[source, m:m + 1, :], (SAMPLES, LANES))
                sums[m] = sums[m] + jnp.where(chosen, row, 0.0)
        for m in range(count):
            out[me_tp, m] = sums[m]

        @pl.loop(1, n_tp)
        def _(step):
            peer = jnp.bitwise_xor(me_tp, step)
            pltpu.make_async_remote_copy(
                src_ref=out.at[me_tp], dst_ref=out.at[me_tp],
                send_sem=fin_send.at[kind], recv_sem=fin_recv.at[kind],
                device_id=(me_ctx, peer), device_id_type=MESH,
            ).start()

    def final(kind, out):
        wait_bytes(out, n_tp - 1, fin_recv.at[kind])
        total = out[0]
        for source in range(1, n_tp):
            total = total + out[source]
        return total

    ready(0)
    low_in = project(v_in, w_in)
    ready(2)
    low_out = project(v_out, w_out)
    s_io[...] = jnp.concatenate([low_in, low_out], axis=1).reshape(s_io.shape)
    ready(4)
    low_hid = project(v_hid, w_hid)
    pl.semaphore_wait(barrier, n_tp + n_ctx - 2)
    tp_exchange(0, s_io, r_io)

    ready(6)
    low_gate = project(v_gate, w_gate)
    s_hg[...] = jnp.concatenate([low_hid, low_gate], axis=1).reshape(s_hg.shape)
    tp_exchange(1, s_hg, r_hg)

    ready(8)
    low_up = project(v_up, w_up).reshape(n_tp, 2, own // 2, K)
    s_u[...] = jnp.concatenate([low_up[:, 0], low_up[:, 1]], axis=2)
    tp_exchange(2, s_u, r_u)
    ids_copy.wait()

    in_out = tp_total(0, r_io)
    side_in, side_out = in_out[:, :K], in_out[:, K:]
    hid_gate = tp_total(1, r_hg)
    grads_go[pl.ds(0, K), :K] = outer(hid_gate[:, K:], side_in)
    grads_go[pl.ds(K, K), :K] = outer(side_out, hid_gate[:, :K])
    slices(grads_go, gs_go, 2)
    ctx_exchange(0, gs_go, gr_go)

    up_halves = tp_total(2, r_u)
    grads_u[:, :K] = outer(jnp.concatenate([up_halves[:, :K], up_halves[:, K:]], axis=0), side_in)
    slices(grads_u, gs_u, 1)
    ctx_exchange(1, gs_u, gr_u)

    by_sample(0, gr_go, f_go, 2)
    by_sample(1, gr_u, f_u, 1)
    go = final(0, f_go)
    result[0] = go[0]
    result[2] = go[1]
    result[1] = final(1, f_u)[0]

    for kind, send in enumerate((s_io, s_hg, s_u)):
        wait_bytes(send, n_tp - 1, tp_send.at[kind])
    for kind, send in enumerate((gs_go, gs_u)):
        wait_bytes(send, n_ctx - 1, ctx_send.at[kind])
    for kind, send in enumerate((f_go, f_u)):
        wait_bytes(send, n_tp - 1, fin_send.at[kind])


def body(ids, x_in, x_hid, x_gate, x_up, x_out, b_in, b_hid, b_gate, b_up, b_out, *, n_ctx, n_tp):
    tokens, narrow = x_in.shape
    wide = x_hid.shape[1]
    own = tokens // n_tp
    f32, bf16 = jnp.float32, jnp.bfloat16
    dma = pltpu.SemaphoreType.DMA
    return pl.pallas_call(
        functools.partial(kernel, n_ctx, n_tp),
        out_shape=jax.ShapeDtypeStruct((3, SAMPLES, LANES), f32),
        in_specs=[pl.BlockSpec(memory_space=pl.ANY)] * 11,
        out_specs=pl.BlockSpec(memory_space=pltpu.VMEM),
        scratch_shapes=[
            pltpu.SMEM(ids.shape, jnp.int32),
            pltpu.VMEM((tokens, narrow), bf16),
            pltpu.VMEM((tokens, wide), bf16),
            pltpu.VMEM((tokens, wide), bf16),
            pltpu.VMEM((tokens, wide), bf16),
            pltpu.VMEM((tokens, narrow), bf16),
            pltpu.VMEM((K, narrow), bf16),
            pltpu.VMEM((K, wide), bf16),
            pltpu.VMEM((K, wide), bf16),
            pltpu.VMEM((K, wide), bf16),
            pltpu.VMEM((K, narrow), bf16),
            pltpu.VMEM((n_tp, own, LANES), f32),
            pltpu.VMEM((n_tp, own, LANES), f32),
            pltpu.VMEM((n_tp, own // 2, LANES), f32),
            pltpu.VMEM((n_tp, own, LANES), f32),
            pltpu.VMEM((n_tp, own, LANES), f32),
            pltpu.VMEM((n_tp, own // 2, LANES), f32),
            pltpu.VMEM((2 * K, LANES), f32),
            pltpu.VMEM((K, LANES), f32),
            pltpu.VMEM((n_ctx, 2, LANES), f32),
            pltpu.VMEM((n_ctx, 1, LANES), f32),
            pltpu.VMEM((n_ctx, 2, LANES), f32),
            pltpu.VMEM((n_ctx, 1, LANES), f32),
            pltpu.VMEM((n_tp, 2, SAMPLES, LANES), f32),
            pltpu.VMEM((n_tp, 1, SAMPLES, LANES), f32),
            dma, dma((10,)), dma((3,)), dma((3,)), dma((2,)), dma((2,)), dma((2,)), dma((2,)),
        ],
        compiler_params=pltpu.CompilerParams(
            collective_id=0, has_side_effects=True, vmem_limit_bytes=60 * 1024 * 1024
        ),
    )(ids, x_in, x_hid, x_gate, x_up, x_out, b_in.T, b_hid.T, b_gate.T, b_up.T, b_out.T)


def solution(mesh):
    split, rows = P("ctx", "tp"), P("tp", None)
    return jax.shard_map(
        functools.partial(body, n_ctx=mesh.shape["ctx"], n_tp=mesh.shape["tp"]),
        mesh=mesh,
        in_specs=(P(), split, split, split, split, split, rows, rows, rows, rows, rows),
        out_specs=P(None, None, "ctx"),
        check_vma=False,
    )
```

```python
import functools

import jax
import jax.numpy as jnp
from jax import lax
from jax.experimental import pallas as pl
from jax.experimental.pallas import tpu as pltpu
from jax.sharding import PartitionSpec as P

K = 64
SAMPLES = 8
BLOCK = 128
LANES = 128
MESH = pl.DeviceIdType.MESH
HIGHEST = lax.Precision.HIGHEST


def project(data_ref, basis_ref):
    half = data_ref.shape[0] // 2
    basis = basis_ref[...]
    parts = [
        lax.dot_general(
            data_ref[pl.ds(start, half), :], basis, (((1,), (1,)), ((), ())), preferred_element_type=jnp.float32
        )
        for start in (0, half)
    ]
    return jnp.concatenate(parts, axis=0)


def outer(output_side, input_side):
    return lax.dot_general(
        output_side, input_side, (((0,), (0,)), ((), ())), precision=HIGHEST, preferred_element_type=jnp.float32
    )


def wait_bytes(ref, count, sem):
    part = ref.at[pl.ds(0, count)]
    pltpu.make_async_copy(part, part, sem).wait()


def kernel(n_ctx, n_tp, x_ids, x_in, x_hid, x_gate, x_up, x_out, b_in, b_hid, b_gate, b_up, b_out, result,
           ids, v_in, v_hid, v_gate, v_up, v_out, w_in, w_hid, w_gate, w_up, w_out,
           s_io, s_hg, s_u, r_io, r_hg, r_u, grads_go, grads_u, gs_go, gs_u, gr_go, gr_u, f_go, f_u,
           ids_sem, load_sem, tp_send, tp_recv, ctx_send, ctx_recv, fin_send, fin_recv, late_sem, all_sem):
    me_ctx, me_tp = lax.axis_index("ctx"), lax.axis_index("tp")
    tokens = v_in.shape[0]
    own = tokens // n_tp

    loads = []

    def load(src, dst):
        copy = pltpu.make_async_copy(src, dst, load_sem.at[len(loads)])
        copy.start()
        loads.append(copy)

    load(x_in, v_in)
    load(b_in, w_in)
    load(x_out, v_out)
    load(b_out, w_out)
    load(x_hid, v_hid)
    load(b_hid, w_hid)

    barrier = pltpu.get_barrier_semaphore()
    half = n_ctx // 2
    first_half = me_ctx < half

    def signal_ctx(sem, start):
        @pl.loop(start, start + half)
        def _(step):
            pl.semaphore_signal(sem, inc=1, device_id=(jnp.bitwise_xor(me_ctx, step), me_tp), device_id_type=MESH)

    @pl.when(first_half)
    def _():
        signal_ctx(barrier, half)

        @pl.loop(1, half)
        def _(step):
            pl.semaphore_signal(barrier, inc=1, device_id=(jnp.bitwise_xor(me_ctx, step), me_tp), device_id_type=MESH)

    @pl.loop(1, n_tp)
    def _(step):
        pl.semaphore_signal(barrier, inc=1, device_id=(me_ctx, jnp.bitwise_xor(me_tp, step)), device_id_type=MESH)

    load(x_gate, v_gate)
    load(b_gate, w_gate)
    load(x_up, v_up)
    load(b_up, w_up)
    ids_copy = pltpu.make_async_copy(x_ids, ids, ids_sem)
    ids_copy.start()

    def ready(first):
        loads[first].wait()
        loads[first + 1].wait()

    def tp_exchange(kind, send, recv):
        @pl.loop(1, n_tp)
        def _(step):
            peer = jnp.bitwise_xor(me_tp, step)
            pltpu.make_async_remote_copy(
                src_ref=send.at[peer], dst_ref=recv.at[me_tp],
                send_sem=tp_send.at[kind], recv_sem=tp_recv.at[kind],
                device_id=(me_ctx, peer), device_id_type=MESH,
            ).start()

        recv[me_tp] = send[me_tp]

    def tp_total(kind, recv):
        wait_bytes(recv, n_tp - 1, tp_recv.at[kind])
        total = recv[0]
        for source in range(1, n_tp):
            total = total + recv[source]
        return total

    def ctx_exchange(kind, send, recv):
        @pl.loop(1, n_ctx)
        def _(step):
            peer = jnp.bitwise_xor(me_ctx, step)
            pltpu.make_async_remote_copy(
                src_ref=send.at[peer], dst_ref=recv.at[me_ctx],
                send_sem=ctx_send.at[kind], recv_sem=ctx_recv.at[kind],
                device_id=(peer, me_tp), device_id_type=MESH,
            ).start()

        recv[me_ctx] = send[me_ctx]

    def slices(grads, send, count):
        even = grads[pl.ds(0, count * K // 2, stride=2), :]
        odd = grads[pl.ds(1, count * K // 2, stride=2), :]
        both = jnp.concatenate([even[:, :K], odd[:, :K]], axis=1)
        for m in range(count):
            send[:, m, :] = both[m * n_ctx:(m + 1) * n_ctx]

    def by_sample(kind, recv, out, count):
        wait_bytes(recv, n_ctx - 1, ctx_recv.at[kind])
        sample = lax.broadcasted_iota(jnp.int32, (SAMPLES, LANES), 0)
        sums = [jnp.zeros((SAMPLES, LANES), jnp.float32) for _ in range(count)]
        blocks = tokens // BLOCK
        mine = me_tp * own // BLOCK
        for source in range(n_ctx):
            chosen = sample == ids[source * blocks + mine]
            for m in range(count):
                row = jnp.broadcast_to(recv[source, m:m + 1, :], (SAMPLES, LANES))
                sums[m] = sums[m] + jnp.where(chosen, row, 0.0)
        for m in range(count):
            out[me_tp, m] = sums[m]

        @pl.loop(1, n_tp)
        def _(step):
            peer = jnp.bitwise_xor(me_tp, step)
            pltpu.make_async_remote_copy(
                src_ref=out.at[me_tp], dst_ref=out.at[me_tp],
                send_sem=fin_send.at[kind], recv_sem=fin_recv.at[kind],
                device_id=(me_ctx, peer), device_id_type=MESH,
            ).start()

    def final(kind, out):
        wait_bytes(out, n_tp - 1, fin_recv.at[kind])
        total = out[0]
        for source in range(1, n_tp):
            total = total + out[source]
        return total

    ready(0)
    low_in = project(v_in, w_in)
    ready(2)
    low_out = project(v_out, w_out)
    s_io[...] = jnp.concatenate([low_in, low_out], axis=1).reshape(s_io.shape)

    @pl.when(first_half)
    def _():
        pl.semaphore_wait(barrier, n_tp - 1 + half - 1)

    @pl.when(jnp.logical_not(first_half))
    def _():
        pl.semaphore_wait(barrier, n_tp - 1 + half)
        signal_ctx(late_sem, half)

    tp_exchange(0, s_io, r_io)
    ready(4)
    low_hid = project(v_hid, w_hid)

    ready(6)
    low_gate = project(v_gate, w_gate)
    s_hg[...] = jnp.concatenate([low_hid, low_gate], axis=1).reshape(s_hg.shape)
    tp_exchange(1, s_hg, r_hg)

    ready(8)
    low_up = project(v_up, w_up).reshape(n_tp, 2, own // 2, K)
    s_u[...] = jnp.concatenate([low_up[:, 0], low_up[:, 1]], axis=2)
    tp_exchange(2, s_u, r_u)
    ids_copy.wait()

    @pl.when(first_half)
    def _():
        pl.semaphore_wait(late_sem, half)
        pl.semaphore_signal(
            all_sem, inc=1, device_id=(n_ctx - 4 - me_ctx + 2 * lax.rem(me_ctx, 4), me_tp), device_id_type=MESH
        )

    in_out = tp_total(0, r_io)
    side_in, side_out = in_out[:, :K], in_out[:, K:]
    hid_gate = tp_total(1, r_hg)
    grads_go[pl.ds(0, K), :K] = outer(hid_gate[:, K:], side_in)
    grads_go[pl.ds(K, K), :K] = outer(side_out, hid_gate[:, :K])
    slices(grads_go, gs_go, 2)
    @pl.when(jnp.logical_not(first_half))
    def _():
        pl.semaphore_wait(all_sem, 1)

    ctx_exchange(0, gs_go, gr_go)

    up_halves = tp_total(2, r_u)
    grads_u[:, :K] = outer(jnp.concatenate([up_halves[:, :K], up_halves[:, K:]], axis=0), side_in)
    slices(grads_u, gs_u, 1)
    ctx_exchange(1, gs_u, gr_u)

    by_sample(0, gr_go, f_go, 2)
    by_sample(1, gr_u, f_u, 1)
    go = final(0, f_go)
    result[0] = go[0]
    result[2] = go[1]
    result[1] = final(1, f_u)[0]

    for kind, send in enumerate((s_io, s_hg, s_u)):
        wait_bytes(send, n_tp - 1, tp_send.at[kind])
    for kind, send in enumerate((gs_go, gs_u)):
        wait_bytes(send, n_ctx - 1, ctx_send.at[kind])
    for kind, send in enumerate((f_go, f_u)):
        wait_bytes(send, n_tp - 1, fin_send.at[kind])


def body(ids, x_in, x_hid, x_gate, x_up, x_out, b_in, b_hid, b_gate, b_up, b_out, *, n_ctx, n_tp):
    tokens, narrow = x_in.shape
    wide = x_hid.shape[1]
    own = tokens // n_tp
    f32, bf16 = jnp.float32, jnp.bfloat16
    dma, plain = pltpu.SemaphoreType.DMA, pltpu.SemaphoreType.REGULAR
    return pl.pallas_call(
        functools.partial(kernel, n_ctx, n_tp),
        out_shape=jax.ShapeDtypeStruct((3, SAMPLES, LANES), f32),
        in_specs=[pl.BlockSpec(memory_space=pl.ANY)] * 11,
        out_specs=pl.BlockSpec(memory_space=pltpu.VMEM),
        scratch_shapes=[
            pltpu.SMEM(ids.shape, jnp.int32),
            pltpu.VMEM((tokens, narrow), bf16),
            pltpu.VMEM((tokens, wide), bf16),
            pltpu.VMEM((tokens, wide), bf16),
            pltpu.VMEM((tokens, wide), bf16),
            pltpu.VMEM((tokens, narrow), bf16),
            pltpu.VMEM((K, narrow), bf16),
            pltpu.VMEM((K, wide), bf16),
            pltpu.VMEM((K, wide), bf16),
            pltpu.VMEM((K, wide), bf16),
            pltpu.VMEM((K, narrow), bf16),
            pltpu.VMEM((n_tp, own, LANES), f32),
            pltpu.VMEM((n_tp, own, LANES), f32),
            pltpu.VMEM((n_tp, own // 2, LANES), f32),
            pltpu.VMEM((n_tp, own, LANES), f32),
            pltpu.VMEM((n_tp, own, LANES), f32),
            pltpu.VMEM((n_tp, own // 2, LANES), f32),
            pltpu.VMEM((2 * K, LANES), f32),
            pltpu.VMEM((K, LANES), f32),
            pltpu.VMEM((n_ctx, 2, LANES), f32),
            pltpu.VMEM((n_ctx, 1, LANES), f32),
            pltpu.VMEM((n_ctx, 2, LANES), f32),
            pltpu.VMEM((n_ctx, 1, LANES), f32),
            pltpu.VMEM((n_tp, 2, SAMPLES, LANES), f32),
            pltpu.VMEM((n_tp, 1, SAMPLES, LANES), f32),
            dma, dma((10,)), dma((3,)), dma((3,)), dma((2,)), dma((2,)), dma((2,)), dma((2,)), plain, plain,
        ],
        compiler_params=pltpu.CompilerParams(
            collective_id=0, has_side_effects=True, vmem_limit_bytes=60 * 1024 * 1024
        ),
    )(ids, x_in, x_hid, x_gate, x_up, x_out, b_in.T, b_hid.T, b_gate.T, b_up.T, b_out.T)


def solution(mesh):
    split, rows = P("ctx", "tp"), P("tp", None)
    return jax.shard_map(
        functools.partial(body, n_ctx=mesh.shape["ctx"], n_tp=mesh.shape["tp"]),
        mesh=mesh,
        in_specs=(P(), split, split, split, split, split, rows, rows, rows, rows, rows),
        out_specs=P(None, None, "ctx"),
        check_vma=False,
    )
```

```python
import functools

import jax
import jax.numpy as jnp
from jax import lax
from jax.experimental import pallas as pl
from jax.experimental.pallas import tpu as pltpu
from jax.sharding import PartitionSpec as P

K = 64
SAMPLES = 8
BLOCK = 128
LANES = 128
TP_ORDER = (6, 7, 5, 2, 3, 1, 4)
MESH = pl.DeviceIdType.MESH
HIGHEST = lax.Precision.HIGHEST


def distant(step):
    z, rest = step // 4, step % 4
    return (4, 5, 3, 2, 6, 7, 1, 0).index(z), -rest


def project(data_ref, basis_ref):
    half = data_ref.shape[0] // 2
    basis = basis_ref[...]
    parts = [
        lax.dot_general(
            data_ref[pl.ds(start, half), :], basis, (((1,), (1,)), ((), ())), preferred_element_type=jnp.float32
        )
        for start in (0, half)
    ]
    return jnp.concatenate(parts, axis=0)


def outer(output_side, input_side):
    return lax.dot_general(
        output_side, input_side, (((0,), (0,)), ((), ())), precision=HIGHEST, preferred_element_type=jnp.float32
    )


def wait_bytes(ref, count, sem):
    part = ref.at[pl.ds(0, count)]
    pltpu.make_async_copy(part, part, sem).wait()


def kernel(n_ctx, n_tp, x_ids, x_in, x_hid, x_gate, x_up, x_out, b_in, b_hid, b_gate, b_up, b_out, result,
           ids, v_in, v_hid, v_gate, v_up, v_out, w_in, w_hid, w_gate, w_up, w_out,
           s_io, s_hg, s_u, r_io, r_hg, r_u, grads_go, grads_u, gs_go, gs_u, gr_go, gr_u, f_go, f_u,
           ids_sem, load_sem, tp_send, tp_recv, ctx_send, ctx_recv, fin_send, fin_recv, late_sem, all_sem):
    me_ctx, me_tp = lax.axis_index("ctx"), lax.axis_index("tp")
    tokens = v_in.shape[0]
    own = tokens // n_tp

    barrier = pltpu.get_barrier_semaphore()

    @pl.loop(1, n_tp)
    def _(step):
        pl.semaphore_signal(barrier, inc=1, device_id=(me_ctx, jnp.bitwise_xor(me_tp, step)), device_id_type=MESH)

    loads = []

    def load(src, dst):
        copy = pltpu.make_async_copy(src, dst, load_sem.at[len(loads)])
        copy.start()
        loads.append(copy)

    load(x_in, v_in)
    load(b_in, w_in)
    load(x_out, v_out)
    load(b_out, w_out)
    load(x_hid, v_hid)
    load(b_hid, w_hid)

    half = n_ctx // 2
    first_half = me_ctx < half

    def signal_ctx(sem, start):
        @pl.loop(start, start + half)
        def _(step):
            pl.semaphore_signal(sem, inc=1, device_id=(jnp.bitwise_xor(me_ctx, step), me_tp), device_id_type=MESH)

    @pl.when(first_half)
    def _():
        signal_ctx(barrier, half)

        @pl.loop(1, half)
        def _(step):
            pl.semaphore_signal(barrier, inc=1, device_id=(jnp.bitwise_xor(me_ctx, step), me_tp), device_id_type=MESH)

    load(x_gate, v_gate)
    load(b_gate, w_gate)
    load(x_up, v_up)
    load(b_up, w_up)
    ids_copy = pltpu.make_async_copy(x_ids, ids, ids_sem)
    ids_copy.start()

    def ready(first):
        loads[first].wait()
        loads[first + 1].wait()

    def tp_exchange(kind, send, recv):
        for step in TP_ORDER:
            peer = jnp.bitwise_xor(me_tp, step)
            pltpu.make_async_remote_copy(
                src_ref=send.at[peer], dst_ref=recv.at[me_tp],
                send_sem=tp_send.at[kind], recv_sem=tp_recv.at[kind],
                device_id=(me_ctx, peer), device_id_type=MESH,
            ).start()

        recv[me_tp] = send[me_tp]

    def tp_total(kind, recv):
        wait_bytes(recv, n_tp - 1, tp_recv.at[kind])
        total = recv[0]
        for source in range(1, n_tp):
            total = total + recv[source]
        return total

    def ctx_exchange(kind, send, recv):
        for step in sorted(range(1, n_ctx), key=distant):
            peer = jnp.bitwise_xor(me_ctx, step)
            pltpu.make_async_remote_copy(
                src_ref=send.at[peer], dst_ref=recv.at[me_ctx],
                send_sem=ctx_send.at[kind], recv_sem=ctx_recv.at[kind],
                device_id=(peer, me_tp), device_id_type=MESH,
            ).start()

        recv[me_ctx] = send[me_ctx]

    def slices(grads, send, count):
        even = grads[pl.ds(0, count * K // 2, stride=2), :]
        odd = grads[pl.ds(1, count * K // 2, stride=2), :]
        both = jnp.concatenate([even[:, :K], odd[:, :K]], axis=1)
        for m in range(count):
            send[:, m, :] = both[m * n_ctx:(m + 1) * n_ctx]

    def by_sample(kind, recv, out, count):
        wait_bytes(recv, n_ctx - 1, ctx_recv.at[kind])
        sample = lax.broadcasted_iota(jnp.int32, (SAMPLES, LANES), 0)
        sums = [jnp.zeros((SAMPLES, LANES), jnp.float32) for _ in range(count)]
        blocks = tokens // BLOCK
        mine = me_tp * own // BLOCK
        for source in range(n_ctx):
            chosen = sample == ids[source * blocks + mine]
            for m in range(count):
                row = jnp.broadcast_to(recv[source, m:m + 1, :], (SAMPLES, LANES))
                sums[m] = sums[m] + jnp.where(chosen, row, 0.0)
        for m in range(count):
            out[me_tp, m] = sums[m]

        for step in TP_ORDER:
            peer = jnp.bitwise_xor(me_tp, step)
            pltpu.make_async_remote_copy(
                src_ref=out.at[me_tp], dst_ref=out.at[me_tp],
                send_sem=fin_send.at[kind], recv_sem=fin_recv.at[kind],
                device_id=(me_ctx, peer), device_id_type=MESH,
            ).start()

    def final(kind, out):
        wait_bytes(out, n_tp - 1, fin_recv.at[kind])
        total = out[0]
        for source in range(1, n_tp):
            total = total + out[source]
        return total

    ready(0)
    low_in = project(v_in, w_in)
    ready(2)
    low_out = project(v_out, w_out)
    s_io[...] = jnp.concatenate([low_in, low_out], axis=1).reshape(s_io.shape)

    @pl.when(first_half)
    def _():
        pl.semaphore_wait(barrier, n_tp - 1 + half - 1)

    @pl.when(jnp.logical_not(first_half))
    def _():
        pl.semaphore_wait(barrier, n_tp - 1 + half)
        signal_ctx(late_sem, half)

    tp_exchange(0, s_io, r_io)
    ready(4)
    low_hid = project(v_hid, w_hid)

    ready(6)
    low_gate = project(v_gate, w_gate)
    s_hg[...] = jnp.concatenate([low_hid, low_gate], axis=1).reshape(s_hg.shape)
    tp_exchange(1, s_hg, r_hg)

    ready(8)
    low_up = project(v_up, w_up).reshape(n_tp, 2, own // 2, K)
    s_u[...] = jnp.concatenate([low_up[:, 0], low_up[:, 1]], axis=2)
    tp_exchange(2, s_u, r_u)
    ids_copy.wait()

    @pl.when(first_half)
    def _():
        pl.semaphore_wait(late_sem, half)
        pl.semaphore_signal(
            all_sem, inc=1, device_id=(n_ctx - 4 - me_ctx + 2 * lax.rem(me_ctx, 4), me_tp), device_id_type=MESH
        )

    in_out = tp_total(0, r_io)
    side_in, side_out = in_out[:, :K], in_out[:, K:]
    hid_gate = tp_total(1, r_hg)
    grads_go[pl.ds(0, K), :K] = outer(hid_gate[:, K:], side_in)
    grads_go[pl.ds(K, K), :K] = outer(side_out, hid_gate[:, :K])
    slices(grads_go, gs_go, 2)
    @pl.when(jnp.logical_not(first_half))
    def _():
        pl.semaphore_wait(all_sem, 1)

    ctx_exchange(0, gs_go, gr_go)

    up_halves = tp_total(2, r_u)
    grads_u[:, :K] = outer(jnp.concatenate([up_halves[:, :K], up_halves[:, K:]], axis=0), side_in)
    slices(grads_u, gs_u, 1)
    ctx_exchange(1, gs_u, gr_u)

    by_sample(0, gr_go, f_go, 2)
    by_sample(1, gr_u, f_u, 1)
    go = final(0, f_go)
    result[0] = go[0]
    result[2] = go[1]
    result[1] = final(1, f_u)[0]

    for kind, send in enumerate((s_io, s_hg, s_u)):
        wait_bytes(send, n_tp - 1, tp_send.at[kind])
    for kind, send in enumerate((gs_go, gs_u)):
        wait_bytes(send, n_ctx - 1, ctx_send.at[kind])
    for kind, send in enumerate((f_go, f_u)):
        wait_bytes(send, n_tp - 1, fin_send.at[kind])


def body(ids, x_in, x_hid, x_gate, x_up, x_out, b_in, b_hid, b_gate, b_up, b_out, *, n_ctx, n_tp):
    tokens, narrow = x_in.shape
    wide = x_hid.shape[1]
    own = tokens // n_tp
    f32, bf16 = jnp.float32, jnp.bfloat16
    dma, plain = pltpu.SemaphoreType.DMA, pltpu.SemaphoreType.REGULAR
    return pl.pallas_call(
        functools.partial(kernel, n_ctx, n_tp),
        out_shape=jax.ShapeDtypeStruct((3, SAMPLES, LANES), f32),
        in_specs=[pl.BlockSpec(memory_space=pl.ANY)] * 11,
        out_specs=pl.BlockSpec(memory_space=pltpu.VMEM),
        scratch_shapes=[
            pltpu.SMEM(ids.shape, jnp.int32),
            pltpu.VMEM((tokens, narrow), bf16),
            pltpu.VMEM((tokens, wide), bf16),
            pltpu.VMEM((tokens, wide), bf16),
            pltpu.VMEM((tokens, wide), bf16),
            pltpu.VMEM((tokens, narrow), bf16),
            pltpu.VMEM((K, narrow), bf16),
            pltpu.VMEM((K, wide), bf16),
            pltpu.VMEM((K, wide), bf16),
            pltpu.VMEM((K, wide), bf16),
            pltpu.VMEM((K, narrow), bf16),
            pltpu.VMEM((n_tp, own, LANES), f32),
            pltpu.VMEM((n_tp, own, LANES), f32),
            pltpu.VMEM((n_tp, own // 2, LANES), f32),
            pltpu.VMEM((n_tp, own, LANES), f32),
            pltpu.VMEM((n_tp, own, LANES), f32),
            pltpu.VMEM((n_tp, own // 2, LANES), f32),
            pltpu.VMEM((2 * K, LANES), f32),
            pltpu.VMEM((K, LANES), f32),
            pltpu.VMEM((n_ctx, 2, LANES), f32),
            pltpu.VMEM((n_ctx, 1, LANES), f32),
            pltpu.VMEM((n_ctx, 2, LANES), f32),
            pltpu.VMEM((n_ctx, 1, LANES), f32),
            pltpu.VMEM((n_tp, 2, SAMPLES, LANES), f32),
            pltpu.VMEM((n_tp, 1, SAMPLES, LANES), f32),
            dma, dma((10,)), dma((3,)), dma((3,)), dma((2,)), dma((2,)), dma((2,)), dma((2,)), plain, plain,
        ],
        compiler_params=pltpu.CompilerParams(
            collective_id=0, has_side_effects=True, vmem_limit_bytes=60 * 1024 * 1024
        ),
    )(ids, x_in, x_hid, x_gate, x_up, x_out, b_in.T, b_hid.T, b_gate.T, b_up.T, b_out.T)


def solution(mesh):
    split, rows = P("ctx", "tp"), P("tp", None)
    return jax.shard_map(
        functools.partial(body, n_ctx=mesh.shape["ctx"], n_tp=mesh.shape["tp"]),
        mesh=mesh,
        in_specs=(P(), split, split, split, split, split, rows, rows, rows, rows, rows),
        out_specs=P(None, None, "ctx"),
        check_vma=False,
    )
```

```python
import functools

import jax
import jax.numpy as jnp
from jax import lax
from jax.experimental import pallas as pl
from jax.experimental.pallas import tpu as pltpu
from jax.sharding import PartitionSpec as P

K = 64
SAMPLES = 8
BLOCK = 128
LANES = 128
TP_ORDER = (6, 7, 5, 2, 3, 1, 4)
MESH = pl.DeviceIdType.MESH
HIGHEST = lax.Precision.HIGHEST


def distant(step):
    z, rest = step // 4, step % 4
    return (4, 5, 3, 2, 6, 7, 1, 0).index(z), -rest


def project(data_ref, basis_ref):
    half = data_ref.shape[0] // 2
    basis = basis_ref[...]
    parts = [
        lax.dot_general(
            data_ref[pl.ds(start, half), :], basis, (((1,), (1,)), ((), ())), preferred_element_type=jnp.float32
        )
        for start in (0, half)
    ]
    return jnp.concatenate(parts, axis=0)


def outer(output_side, input_side):
    wide, narrow = zip(*[
        (side.astype(jnp.bfloat16), (side - side.astype(jnp.bfloat16).astype(jnp.float32)).astype(jnp.bfloat16))
        for side in (output_side, input_side)
    ])
    return lax.dot_general(
        jnp.concatenate([wide[0], wide[0], narrow[0]], axis=0),
        jnp.concatenate([wide[1], narrow[1], wide[1]], axis=0),
        (((0,), (0,)), ((), ())),
        preferred_element_type=jnp.float32,
    )


def wait_bytes(ref, count, sem):
    part = ref.at[pl.ds(0, count)]
    pltpu.make_async_copy(part, part, sem).wait()


def kernel(n_ctx, n_tp, x_ids, x_in, x_hid, x_gate, x_up, x_out, b_in, b_hid, b_gate, b_up, b_out, result,
           ids, v_in, v_hid, v_gate, v_up, v_out, w_in, w_hid, w_gate, w_up, w_out,
           s_io, s_hg, s_u, r_io, r_hg, r_u, grads_go, grads_u, gs_go, gs_u, gr_go, gr_u, f_go, f_u,
           ids_sem, load_sem, tp_send, tp_recv, ctx_send, ctx_recv, fin_send, fin_recv, late_sem, all_sem):
    me_ctx, me_tp = lax.axis_index("ctx"), lax.axis_index("tp")
    tokens = v_in.shape[0]
    own = tokens // n_tp

    barrier = pltpu.get_barrier_semaphore()

    for step in TP_ORDER:
        pl.semaphore_signal(barrier, inc=1, device_id=(me_ctx, jnp.bitwise_xor(me_tp, step)), device_id_type=MESH)

    loads = []

    def load(src, dst):
        copy = pltpu.make_async_copy(src, dst, load_sem.at[len(loads)])
        copy.start()
        loads.append(copy)

    load(x_in, v_in)
    load(b_in, w_in)
    load(x_out, v_out)
    load(b_out, w_out)
    load(x_hid, v_hid)
    load(b_hid, w_hid)

    half = n_ctx // 2
    first_half = me_ctx < half

    def signal_ctx(sem, start):
        for step in sorted(range(start, start + half), key=distant):
            pl.semaphore_signal(sem, inc=1, device_id=(jnp.bitwise_xor(me_ctx, step), me_tp), device_id_type=MESH)

    @pl.when(first_half)
    def _():
        signal_ctx(barrier, half)

        @pl.loop(1, half)
        def _(step):
            pl.semaphore_signal(barrier, inc=1, device_id=(jnp.bitwise_xor(me_ctx, step), me_tp), device_id_type=MESH)

    load(x_gate, v_gate)
    load(b_gate, w_gate)
    load(x_up, v_up)
    load(b_up, w_up)
    ids_copy = pltpu.make_async_copy(x_ids, ids, ids_sem)
    ids_copy.start()

    def ready(first):
        loads[first].wait()
        loads[first + 1].wait()

    def tp_exchange(kind, send, recv):
        for step in TP_ORDER:
            peer = jnp.bitwise_xor(me_tp, step)
            pltpu.make_async_remote_copy(
                src_ref=send.at[peer], dst_ref=recv.at[me_tp],
                send_sem=tp_send.at[kind], recv_sem=tp_recv.at[kind],
                device_id=(me_ctx, peer), device_id_type=MESH,
            ).start()

        recv[me_tp] = send[me_tp]

    def tp_total(kind, recv):
        wait_bytes(recv, n_tp - 1, tp_recv.at[kind])
        total = recv[0]
        for source in range(1, n_tp):
            total = total + recv[source]
        return total

    def ctx_exchange(kind, send, recv):
        for step in sorted(range(1, n_ctx), key=distant):
            peer = jnp.bitwise_xor(me_ctx, step)
            pltpu.make_async_remote_copy(
                src_ref=send.at[peer], dst_ref=recv.at[me_ctx],
                send_sem=ctx_send.at[kind], recv_sem=ctx_recv.at[kind],
                device_id=(peer, me_tp), device_id_type=MESH,
            ).start()

        recv[me_ctx] = send[me_ctx]

    def slices(grads, send, count):
        even = grads[pl.ds(0, count * K // 2, stride=2), :]
        odd = grads[pl.ds(1, count * K // 2, stride=2), :]
        both = jnp.concatenate([even[:, :K], odd[:, :K]], axis=1)
        for m in range(count):
            send[:, m, :] = both[m * n_ctx:(m + 1) * n_ctx]

    def by_sample(kind, recv, out, count):
        wait_bytes(recv, n_ctx - 1, ctx_recv.at[kind])
        sample = lax.broadcasted_iota(jnp.int32, (SAMPLES, LANES), 0)
        sums = [jnp.zeros((SAMPLES, LANES), jnp.float32) for _ in range(count)]
        blocks = tokens // BLOCK
        mine = me_tp * own // BLOCK
        for source in range(n_ctx):
            chosen = sample == ids[source * blocks + mine]
            for m in range(count):
                row = jnp.broadcast_to(recv[source, m:m + 1, :], (SAMPLES, LANES))
                sums[m] = sums[m] + jnp.where(chosen, row, 0.0)
        for m in range(count):
            out[me_tp, m] = sums[m]

        for step in TP_ORDER:
            peer = jnp.bitwise_xor(me_tp, step)
            pltpu.make_async_remote_copy(
                src_ref=out.at[me_tp], dst_ref=out.at[me_tp],
                send_sem=fin_send.at[kind], recv_sem=fin_recv.at[kind],
                device_id=(me_ctx, peer), device_id_type=MESH,
            ).start()

    def final(kind, out):
        wait_bytes(out, n_tp - 1, fin_recv.at[kind])
        total = out[0]
        for source in range(1, n_tp):
            total = total + out[source]
        return total

    ready(0)
    low_in = project(v_in, w_in)
    ready(2)
    low_out = project(v_out, w_out)
    s_io[...] = jnp.concatenate([low_in, low_out], axis=1).reshape(s_io.shape)

    @pl.when(first_half)
    def _():
        pl.semaphore_wait(barrier, n_tp - 1 + half - 1)

    @pl.when(jnp.logical_not(first_half))
    def _():
        pl.semaphore_wait(barrier, n_tp - 1 + half)
        signal_ctx(late_sem, half)

    tp_exchange(0, s_io, r_io)
    ready(4)
    low_hid = project(v_hid, w_hid)

    ready(6)
    low_gate = project(v_gate, w_gate)
    s_hg[...] = jnp.concatenate([low_hid, low_gate], axis=1).reshape(s_hg.shape)
    tp_exchange(1, s_hg, r_hg)

    ready(8)
    low_up = project(v_up, w_up).reshape(n_tp, 2, own // 2, K)
    s_u[...] = jnp.concatenate([low_up[:, 0], low_up[:, 1]], axis=2)
    tp_exchange(2, s_u, r_u)
    ids_copy.wait()

    @pl.when(first_half)
    def _():
        pl.semaphore_wait(late_sem, half)
        pl.semaphore_signal(
            all_sem, inc=1, device_id=(n_ctx - 4 - me_ctx + 2 * lax.rem(me_ctx, 4), me_tp), device_id_type=MESH
        )

    in_out = tp_total(0, r_io)
    side_in, side_out = in_out[:, :K], in_out[:, K:]
    hid_gate = tp_total(1, r_hg)
    grads_go[pl.ds(0, K), :K] = outer(hid_gate[:, K:], side_in)
    grads_go[pl.ds(K, K), :K] = outer(side_out, hid_gate[:, :K])
    slices(grads_go, gs_go, 2)
    @pl.when(jnp.logical_not(first_half))
    def _():
        pl.semaphore_wait(all_sem, 1)

    ctx_exchange(0, gs_go, gr_go)

    up_halves = tp_total(2, r_u)
    grads_u[:, :K] = outer(jnp.concatenate([up_halves[:, :K], up_halves[:, K:]], axis=0), side_in)
    slices(grads_u, gs_u, 1)
    ctx_exchange(1, gs_u, gr_u)

    by_sample(0, gr_go, f_go, 2)
    by_sample(1, gr_u, f_u, 1)
    go = final(0, f_go)
    result[0] = go[0]
    result[2] = go[1]
    result[1] = final(1, f_u)[0]

    for kind, send in enumerate((s_io, s_hg, s_u)):
        wait_bytes(send, n_tp - 1, tp_send.at[kind])
    for kind, send in enumerate((gs_go, gs_u)):
        wait_bytes(send, n_ctx - 1, ctx_send.at[kind])
    for kind, send in enumerate((f_go, f_u)):
        wait_bytes(send, n_tp - 1, fin_send.at[kind])


def body(ids, x_in, x_hid, x_gate, x_up, x_out, b_in, b_hid, b_gate, b_up, b_out, *, n_ctx, n_tp):
    tokens, narrow = x_in.shape
    wide = x_hid.shape[1]
    own = tokens // n_tp
    f32, bf16 = jnp.float32, jnp.bfloat16
    dma, plain = pltpu.SemaphoreType.DMA, pltpu.SemaphoreType.REGULAR
    return pl.pallas_call(
        functools.partial(kernel, n_ctx, n_tp),
        out_shape=jax.ShapeDtypeStruct((3, SAMPLES, LANES), f32),
        in_specs=[pl.BlockSpec(memory_space=pl.ANY)] * 11,
        out_specs=pl.BlockSpec(memory_space=pltpu.VMEM),
        scratch_shapes=[
            pltpu.SMEM(ids.shape, jnp.int32),
            pltpu.VMEM((tokens, narrow), bf16),
            pltpu.VMEM((tokens, wide), bf16),
            pltpu.VMEM((tokens, wide), bf16),
            pltpu.VMEM((tokens, wide), bf16),
            pltpu.VMEM((tokens, narrow), bf16),
            pltpu.VMEM((K, narrow), bf16),
            pltpu.VMEM((K, wide), bf16),
            pltpu.VMEM((K, wide), bf16),
            pltpu.VMEM((K, wide), bf16),
            pltpu.VMEM((K, narrow), bf16),
            pltpu.VMEM((n_tp, own, LANES), f32),
            pltpu.VMEM((n_tp, own, LANES), f32),
            pltpu.VMEM((n_tp, own // 2, LANES), f32),
            pltpu.VMEM((n_tp, own, LANES), f32),
            pltpu.VMEM((n_tp, own, LANES), f32),
            pltpu.VMEM((n_tp, own // 2, LANES), f32),
            pltpu.VMEM((2 * K, LANES), f32),
            pltpu.VMEM((K, LANES), f32),
            pltpu.VMEM((n_ctx, 2, LANES), f32),
            pltpu.VMEM((n_ctx, 1, LANES), f32),
            pltpu.VMEM((n_ctx, 2, LANES), f32),
            pltpu.VMEM((n_ctx, 1, LANES), f32),
            pltpu.VMEM((n_tp, 2, SAMPLES, LANES), f32),
            pltpu.VMEM((n_tp, 1, SAMPLES, LANES), f32),
            dma, dma((10,)), dma((3,)), dma((3,)), dma((2,)), dma((2,)), dma((2,)), dma((2,)), plain, plain,
        ],
        compiler_params=pltpu.CompilerParams(
            collective_id=0, has_side_effects=True, vmem_limit_bytes=60 * 1024 * 1024
        ),
    )(ids, x_in, x_hid, x_gate, x_up, x_out, b_in.T, b_hid.T, b_gate.T, b_up.T, b_out.T)


def solution(mesh):
    split, rows = P("ctx", "tp"), P("tp", None)
    return jax.shard_map(
        functools.partial(body, n_ctx=mesh.shape["ctx"], n_tp=mesh.shape["tp"]),
        mesh=mesh,
        in_specs=(P(), split, split, split, split, split, rows, rows, rows, rows, rows),
        out_specs=P(None, None, "ctx"),
        check_vma=False,
    )
```
